32 devices in a mesh: el: 4 (over x, core), tg: 8 (over z, y).
Axes of the slice: x: 2, y: 2, z: 4, core: 2. Of those that a mesh axis runs over, the one named last changes fastest.
Arguments:
- field_points: bfloat16 [16384, 16, 256], P(('el', 'tg')), may hold values from -6 to 6
- owner_map: int32 [32, 512], P(('el', 'tg')), may hold values from 0 to 31, as said below
- send_counts: int32 [32, 512], P(('el', 'tg')), may hold values from 15 to 16
- tile_rows: int32 [32, 32], P(('el', 'tg')), may hold values from 0 to 31, each once within a row
- tile_cols: int32 [32, 32, 16], P(('el', 'tg')), may hold values from 0 to 63, as said below
- weights: bfloat16 [32, 32, 16, 128, 128], P(('el', 'tg')), may hold values from -0.125 to 0.125
Outputs:
- remapped: bfloat16 [256, 131072], P('el', 'tg')
The draws below stay inside these ranges and needn't reach their ends.
Inputs may be any that keep to these rules, and one draw needn't show every extreme that they name: `owner_map`: each device's 512 elements name every owner exactly 16 times. `tile_cols`: the 16 entries of one target tile are distinct.
All inputs are finite; a program needn't handle non-finite values.
Results may differ from the reference program's by a relative error of at most 0.001.
Values may be sent and summed in bfloat16 or wider, within the bound.
A program may use at most 128 MiB of HBM per device.

```python
import jax
import jax.numpy as jnp
from jax import lax

NPTS = 16
TILE = 128
BLOCKS = 16
ELEM_DEV = 512
TTILES = 32
CH = 256
PER_OWNER = 16
LOCAL_TILES = 64
ELEMS = 16384
TGT_ROWS = 131072
N_EL = 4
N_TG = 8
DEVICES = 32


def owner_table(key):
    keys = jax.random.split(jax.random.fold_in(key, 11), DEVICES)
    shuffled = jax.vmap(lambda single: jax.random.permutation(single, ELEM_DEV))(keys)
    return (shuffled % DEVICES).astype(jnp.int32)


def draw_owner_map(key, part):
    return owner_table(key)


def draw_send_counts(key, part):
    owners = owner_table(key)
    full_owner = jax.random.randint(jax.random.fold_in(key, 12), (DEVICES,), 0, DEVICES)
    base_counts = jax.random.randint(jax.random.fold_in(key, 13), (DEVICES, ELEM_DEV), 15, NPTS + 1)
    return jnp.where(owners == full_owner[:, None], NPTS, base_counts).astype(jnp.int32)


def draw_tile_cols(key, part):
    keys = jax.random.split(jax.random.fold_in(key, 14), DEVICES * TTILES)
    picks = jax.vmap(lambda single: jax.random.permutation(single, LOCAL_TILES)[:BLOCKS])(keys)
    return picks.reshape(DEVICES, TTILES, BLOCKS).astype(jnp.int32)


def shard_levels(key, dims, cuts, smallest, high):
    gain = 1.0
    for dim, shards_of in cuts:
        steps = jax.random.uniform(jax.random.fold_in(jax.random.fold_in(key, 6), dim), (shards_of,), jnp.float32, smallest / len(cuts), high / len(cuts))
        gain = gain * jnp.repeat(jnp.exp(steps), dims[dim] // shards_of).reshape((-1,) + (1,) * (len(dims) - 1 - dim))
    return gain


def centred(rng, extent, spread, limit, shards=(), kind=jnp.bfloat16):
    values = jax.random.normal(rng, extent, jnp.float32) * spread
    if len(shards) > 0:
        values = shard_levels(rng, extent, shards, -0.22, 0.18) * values
    return jnp.clip(values, min=-limit, max=limit).astype(kind)


def setup_inputs(seed: int = 0) -> dict:
    seeds = jax.random.split(jax.random.key(seed), 7)
    return {
        "field_points": centred(seeds[0], (ELEMS, NPTS, CH), 1.0, 6.0, ((0, 32),)),
        "owner_map": draw_owner_map(jax.random.fold_in(seeds[6], 71), 0),
        "send_counts": draw_send_counts(jax.random.fold_in(seeds[6], 71), 0),
        "tile_rows": jax.vmap(lambda own: jax.random.permutation(own, TTILES))(jax.random.split(seeds[3], DEVICES)).reshape((DEVICES, TTILES)).astype(jnp.int32),
        "tile_cols": draw_tile_cols(jax.random.fold_in(seeds[6], 71), 0),
        "weights": centred(seeds[5], (DEVICES, TTILES, BLOCKS, TILE, TILE), (BLOCKS * TILE) ** -0.5, 0.125, ((0, 32),)),
    }


def reference(field_points, owner_map, send_counts, tile_rows, tile_cols, weights):
    device_total = N_EL * N_TG
    ordering = jnp.argsort(owner_map, axis=1, stable=True).astype(jnp.int32)
    selected = ordering.reshape(device_total, device_total, PER_OWNER)
    offsets = (jnp.arange(device_total).astype(jnp.int32) * ELEM_DEV).astype(jnp.int32)
    global_ids = (selected + offsets[:, None, None]).astype(jnp.int32)
    flat_counts = send_counts.reshape(-1)
    point_index = jnp.arange(NPTS).astype(jnp.int32)

    def owner_work(owner):
        ids = global_ids[:, owner, :].reshape(-1)
        rows = field_points[ids]
        live_rows = point_index[None, :] < flat_counts[ids][:, None]
        rows = jnp.where(live_rows[:, :, None], rows, jnp.zeros((), rows.dtype))
        source = rows.reshape(LOCAL_TILES, TILE, CH)
        gathered = source[tile_cols[owner]].astype(jnp.float32)
        product = jnp.einsum("tkij,tkjc->cti", weights[owner].astype(jnp.float32), gathered)
        placed = jnp.zeros_like(product).at[:, tile_rows[owner]].set(product)
        return placed.reshape(CH, TTILES * TILE).astype(jnp.bfloat16)

    results = lax.map(owner_work, jnp.arange(device_total).astype(jnp.int32))
    results = results.reshape(N_EL, N_TG, CH, TTILES * TILE)
    return results.transpose(2, 1, 0, 3).reshape(CH, TGT_ROWS)
```

```python
import functools

import jax
import jax.numpy as jnp
from jax import lax
from jax.experimental import pallas as pl
from jax.experimental.pallas import tpu as pltpu
from jax.sharding import PartitionSpec as P

LANES = 128


def kernel(
    n_el, n_tg, per_owner, sel_ref, counts_ref, inv_ref, cols_ref, field_hbm, weights_hbm, out_hbm,
    field, weights, packed, source_far, source_near, mixed, field_sem, weight_sem, own_sem, send_sem, recv_sem,
    swap_send, swap_recv, place_sem,
):
    n = n_el * n_tg
    half_el = n_el // 2
    mesh_id = pl.DeviceIdType.MESH
    my_el = lax.axis_index("el")
    my_tg = lax.axis_index("tg")
    me = my_el * n_tg + my_tg
    points = field.shape[1]
    tiles, blocks = weights.shape[:2]
    tile = weights.shape[2]
    per_half = LANES // half_el
    cells = tiles * tile
    sources = (source_far, source_near)

    field_copy = pltpu.make_async_copy(field_hbm, field, field_sem)
    field_copy.start()
    weight_copy = pltpu.make_async_copy(weights_hbm, weights, weight_sem)

    barrier = pltpu.get_barrier_semaphore()

    def peer(step):
        other = lax.rem(me + step, n)
        return other, (other // n_tg, lax.rem(other, n_tg))

    def greet(step, carry):
        pl.semaphore_signal(barrier, inc=1, device_id=peer(step)[1], device_id_type=mesh_id)
        return carry

    lax.fori_loop(1, n, greet, 0)
    field_copy.wait()

    row = lax.broadcasted_iota(jnp.int32, (points, LANES), 0)

    def pack(other):
        def one(g, carry):
            element = sel_ref[other * per_owner + g]
            live = row < counts_ref[element]
            for h in range(2):
                values = field[element, :, h * LANES:(h + 1) * LANES]
                packed[h, other, g] = jnp.where(live, values, jnp.zeros_like(values))
            return carry

        lax.fori_loop(0, per_owner, one, 0, unroll=min(per_owner, 4))

    def lanes_of(other_el, phase):
        near = other_el // half_el
        return 1 - near if phase == 0 else near

    def send(step, phase):
        other, where = peer(step)
        return pltpu.make_async_remote_copy(
            src_ref=packed.at[lanes_of(where[0], phase), other],
            dst_ref=sources[phase].at[me],
            send_sem=send_sem.at[phase, step],
            recv_sem=recv_sem.at[phase, step],
            device_id=where,
            device_id_type=mesh_id,
        )

    def arrival(step, phase):
        sender = lax.rem(me + n - step, n)
        return pltpu.make_async_copy(packed.at[0, 0], sources[phase].at[sender], recv_sem.at[phase, step])

    pack(lax.rem(me + 1, n))
    pl.semaphore_wait(barrier, n - 1)

    def first(step, carry):
        send(step, 0).start()
        pack(lax.rem(me + step + 1, n))
        return carry

    lax.fori_loop(1, n, first, 0)
    weight_copy.start()
    for phase in range(2):
        pltpu.make_async_copy(packed.at[lanes_of(my_el, phase), me], sources[phase].at[me], own_sem.at[phase]).start()

    def second(step, carry):
        send(step, 0).wait_send()
        send(step, 1).start()
        return carry

    lax.fori_loop(1, n, second, 0)

    def multiply(phase):
        def landed(step, carry):
            arrival(step, phase).wait()
            return carry

        lax.fori_loop(1, n, landed, 0)
        pltpu.make_async_copy(packed.at[0, 0], sources[phase].at[me], own_sem.at[phase]).wait()
        flat = sources[phase].reshape(n * per_owner * points // tile, tile, LANES)

        def one(q, carry):
            t = inv_ref[q]
            left = jnp.concatenate([weights[t, k] for k in range(blocks)], axis=1)
            right = jnp.concatenate([flat[cols_ref[t * blocks + k]] for k in range(blocks)], axis=0)
            product = jnp.dot(left, right, preferred_element_type=jnp.float32)
            start = pl.multiple_of(q * tile, tile)
            mixed[phase, :, pl.ds(start, tile)] = product.T.astype(mixed.dtype)
            return carry

        lax.fori_loop(0, tiles, one, 0)

    my_columns = pl.ds(pl.multiple_of(my_el * cells, cells), cells)
    my_half = my_el // half_el

    def swap(phase, m):
        group = 1 - my_half if phase == 0 else my_half
        index = lax.rem(lax.rem(my_el, half_el) + m, half_el)
        return pltpu.make_async_remote_copy(
            src_ref=mixed.at[phase, pl.ds(pl.multiple_of(index * per_half, per_half), per_half)],
            dst_ref=out_hbm.at[:, my_columns],
            send_sem=swap_send.at[phase, m],
            recv_sem=swap_recv.at[phase, m],
            device_id=(group * half_el + index, my_tg),
            device_id_type=mesh_id,
        )

    def swapped(phase, m):
        group = 1 - my_half if phase == 0 else my_half
        index = lax.rem(lax.rem(my_el, half_el) + half_el - m, half_el)
        columns = pl.ds(pl.multiple_of((group * half_el + index) * cells, cells), cells)
        return pltpu.make_async_copy(
            mixed.at[phase, pl.ds(0, per_half)], out_hbm.at[:, columns], swap_recv.at[phase, m]
        )

    weight_copy.wait()
    multiply(0)
    for m in range(half_el):
        swap(0, m).start()
    multiply(1)
    for m in range(1, half_el):
        swap(1, m).start()
    mine = pl.multiple_of(lax.rem(my_el, half_el) * per_half, per_half)
    place = pltpu.make_async_copy(mixed.at[1, pl.ds(mine, per_half)], out_hbm.at[:, my_columns], place_sem)
    place.start()

    def sent(step, carry):
        send(step, 1).wait_send()
        return carry

    lax.fori_loop(1, n, sent, 0)
    for phase in range(2):
        for m in range(phase, half_el):
            swap(phase, m).wait_send()
            swapped(phase, m).wait()
    place.wait()


def on_device(n_el, n_tg, field_points, owner_map, send_counts, tile_rows, tile_cols, weights):
    elements, points, channels = field_points.shape
    n = n_el * n_tg
    per_owner = elements // n
    _, tiles, blocks, tile, _ = weights.shape
    owner = owner_map[0]
    index = jnp.arange(elements, dtype=jnp.int32)
    same = (owner[:, None] == owner[None, :]) & (index[None, :] < index[:, None])
    slot = owner * per_owner + jnp.sum(same.astype(jnp.int32), axis=1)
    sel = jnp.sum(jnp.where(slot[:, None] == index[None, :], index[:, None], 0), axis=0)
    order = jnp.arange(tiles, dtype=jnp.int32)
    inverse = jnp.sum(jnp.where(tile_rows[0][:, None] == order[None, :], order[:, None], 0), axis=0)
    half_el = n_el // 2
    smem = pl.BlockSpec(memory_space=pltpu.SMEM)
    anywhere = pl.BlockSpec(memory_space=pl.ANY)
    dma = pltpu.SemaphoreType.DMA
    kind = field_points.dtype
    return pl.pallas_call(
        functools.partial(kernel, n_el, n_tg, per_owner),
        out_shape=jax.ShapeDtypeStruct((channels // n_el, n_el * tiles * tile), kind),
        in_specs=[smem] * 4 + [anywhere] * 2,
        out_specs=anywhere,
        scratch_shapes=[
            pltpu.VMEM((elements, points, channels), kind),
            pltpu.VMEM((tiles, blocks, tile, tile), kind),
            pltpu.VMEM((2, n, per_owner, points, LANES), kind),
            pltpu.VMEM((n, per_owner, points, LANES), kind),
            pltpu.VMEM((n, per_owner, points, LANES), kind),
            pltpu.VMEM((2, LANES, tiles * tile), kind),
            dma(()),
            dma(()),
            dma((2,)),
            dma((2, n)),
            dma((2, n)),
            dma((2, half_el)),
            dma((2, half_el)),
            dma(()),
        ],
        compiler_params=pltpu.CompilerParams(
            collective_id=0, has_side_effects=True, vmem_limit_bytes=56 * 2**20
        ),
        cost_estimate=pl.CostEstimate(
            flops=2 * tiles * blocks * tile * tile * channels,
            bytes_accessed=weights.size * 2 + field_points.size * 2,
            transcendentals=0,
        ),
    )(sel, send_counts[0], inverse, tile_cols[0].reshape(-1), field_points, weights[0])


def solution(mesh):
    n_el, n_tg = mesh.shape["el"], mesh.shape["tg"]
    return jax.shard_map(
        functools.partial(on_device, n_el, n_tg),
        mesh=mesh,
        in_specs=(
            P(("el", "tg"), None, None),
            P(("el", "tg"), None),
            P(("el", "tg"), None),
            P(("el", "tg"), None),
            P(("el", "tg"), None, None),
            P(("el", "tg"), None, None, None, None),
        ),
        out_specs=P("el", "tg"),
        check_vma=False,
    )
```

```python
import functools

import jax
import jax.numpy as jnp
from jax import lax
from jax.experimental import pallas as pl
from jax.experimental.pallas import tpu as pltpu
from jax.sharding import PartitionSpec as P

LANES = 128
GROUPS = 4
UNROLL = 2


def kernel(
    n_el, n_tg, per_owner, owner_ref, counts_ref, rows_ref, cols_ref, field_hbm, weights_hbm, out_hbm,
    field, weights, packed, source_far, source_near, mixed, field_sem, weight_sem, own_sem, send_sem, recv_sem,
    swap_send, swap_recv, place_sem, table_vmem, place_vmem, table, place_table, table_sem,
):
    n = n_el * n_tg
    half_el = n_el // 2
    mesh_id = pl.DeviceIdType.MESH
    my_el = lax.axis_index("el")
    my_tg = lax.axis_index("tg")
    me = my_el * n_tg + my_tg
    points = field.shape[1]
    tiles, blocks = weights.shape[:2]
    tile = weights.shape[2]
    per_half = LANES // half_el
    cells = tiles * tile
    sources = (source_far, source_near)

    field_copy = pltpu.make_async_copy(field_hbm, field, field_sem)
    field_copy.start()
    weight_copy = pltpu.make_async_copy(weights_hbm, weights, weight_sem)

    barrier = pltpu.get_barrier_semaphore()

    def offsets(step):
        count = step + 1
        return lax.rem(count // n_tg, n_el), lax.rem(count, n_tg)

    def peer(step):
        el_step, tg_step = offsets(step)
        where = (lax.rem(my_el + el_step, n_el), lax.rem(my_tg + tg_step, n_tg))
        return where[0] * n_tg + where[1], where

    def greet(step, carry):
        pl.semaphore_signal(barrier, inc=1, device_id=peer(step)[1], device_id_type=mesh_id)
        return carry

    lax.fori_loop(0, n - 1, greet, 0)

    slots = table_vmem.shape[0] // 2
    elements = field.shape[0]
    owner = owner_ref[...]
    index = lax.broadcasted_iota(jnp.int32, (1, elements), 1)
    owned = lax.broadcasted_iota(jnp.int32, (table_vmem.shape[1], elements), 0) == owner
    onehot = owned.astype(jnp.float32).astype(jnp.bfloat16)
    earlier = lax.broadcasted_iota(jnp.int32, (elements, elements), 0) < lax.broadcasted_iota(
        jnp.int32, (elements, elements), 1
    )
    before = jnp.dot(onehot, earlier.astype(jnp.float32).astype(jnp.bfloat16), preferred_element_type=jnp.float32)
    rank = jnp.sum(jnp.where(owned, before, 0.0), axis=0, keepdims=True).astype(jnp.int32)
    ranked = lax.broadcasted_iota(jnp.int32, (slots, elements), 0) == rank
    picks = [jnp.where(ranked, x, 0).astype(jnp.float32) for x in (index // LANES, lax.rem(index, LANES), counts_ref[...])]
    found = lax.dot_general(
        jnp.concatenate(picks, axis=0).astype(jnp.bfloat16), onehot, (((1,), (1,)), ((), ())),
        preferred_element_type=jnp.float32,
    ).astype(jnp.int32)
    table_vmem[:slots] = found[:slots] * LANES + found[slots:2 * slots]
    table_vmem[slots:] = found[2 * slots:]
    placed = lax.broadcasted_iota(jnp.int32, (place_vmem.shape[1], tiles), 0) == rows_ref[...]
    order = lax.broadcasted_iota(jnp.int32, (place_vmem.shape[0], tiles), 1)
    place_vmem[...] = lax.dot_general(
        order.astype(jnp.float32).astype(jnp.bfloat16), placed.astype(jnp.float32).astype(jnp.bfloat16),
        (((1,), (1,)), ((), ())), preferred_element_type=jnp.float32,
    ).astype(jnp.int32)
    table_copies = [
        pltpu.make_async_copy(table_vmem, table, table_sem.at[0]),
        pltpu.make_async_copy(place_vmem, place_table, table_sem.at[1]),
    ]
    for copy in table_copies:
        copy.start()
    for copy in table_copies:
        copy.wait()
    field_copy.wait()

    row = lax.broadcasted_iota(jnp.int32, (points, LANES), 0)

    def pack(other):
        def one(g, carry):
            element = jnp.clip(table[g, other], 0, elements - 1)
            live = row < table[slots + g, other]
            for h in range(2):
                values = field[element, :, h * LANES:(h + 1) * LANES]
                packed[h, other, g] = jnp.where(live, values, jnp.zeros_like(values))
            return carry

        lax.fori_loop(0, per_owner, one, 0, unroll=min(per_owner, 4))

    def lanes_of(other_el, phase):
        near = other_el // half_el
        return 1 - near if phase == 0 else near

    def send(step, phase):
        other, where = peer(step)
        return pltpu.make_async_remote_copy(
            src_ref=packed.at[lanes_of(where[0], phase), other],
            dst_ref=sources[phase].at[me],
            send_sem=send_sem.at[phase, step],
            recv_sem=recv_sem.at[phase, step],
            device_id=where,
            device_id_type=mesh_id,
        )

    def arrival(step, phase):
        el_step, tg_step = offsets(step)
        sender = lax.rem(my_el + n_el - el_step, n_el) * n_tg + lax.rem(my_tg + n_tg - tg_step, n_tg)
        return pltpu.make_async_copy(packed.at[0, 0], sources[phase].at[sender], recv_sem.at[phase, step])

    pack(peer(0)[0])
    pl.semaphore_wait(barrier, n - 1)

    def first(step, carry):
        send(step, 0).start()
        pack(peer(step + 1)[0])
        return carry

    lax.fori_loop(0, n - 1, first, 0)
    weight_copy.start()
    for phase in range(2):
        pltpu.make_async_copy(packed.at[lanes_of(my_el, phase), me], sources[phase].at[me], own_sem.at[phase]).start()

    def second(step, carry):
        send(step, 0).wait_send()
        send(step, 1).start()
        return carry

    lax.fori_loop(0, n - 1, second, 0)

    def land(phase):
        def landed(step, carry):
            arrival(step, phase).wait()
            return carry

        lax.fori_loop(0, n - 1, landed, 0)
        pltpu.make_async_copy(packed.at[0, 0], sources[phase].at[me], own_sem.at[phase]).wait()

    def multiply(phase, group):
        flat = sources[phase].reshape(n * per_owner * points // tile, tile, LANES)

        def one(q, carry):
            t = jnp.clip(place_table[0, q], 0, tiles - 1)
            left = jnp.concatenate([weights[t, k] for k in range(blocks)], axis=1)
            right = jnp.concatenate([flat[cols_ref[k, t]] for k in range(blocks)], axis=0)
            product = jnp.dot(left, right, preferred_element_type=jnp.float32)
            start = pl.multiple_of(q * tile, tile)
            mixed[phase, :, pl.ds(start, tile)] = product.T.astype(mixed.dtype)
            return carry

        share = tiles // GROUPS
        lax.fori_loop(group * share, (group + 1) * share, one, 0, unroll=UNROLL)

    piece = cells // GROUPS
    my_half = my_el // half_el
    my_index = lax.rem(my_el, half_el)

    def block(index):
        return pl.ds(pl.multiple_of(index * per_half, per_half), per_half)

    def columns(owner_el, group):
        return pl.ds(pl.multiple_of(owner_el * cells + group * piece, piece), piece)

    def swap(phase, m, group):
        side = 1 - my_half if phase == 0 else my_half
        index = lax.rem(my_index + m, half_el)
        return pltpu.make_async_remote_copy(
            src_ref=mixed.at[phase, block(index), pl.ds(group * piece, piece)],
            dst_ref=out_hbm.at[:, columns(my_el, group)],
            send_sem=swap_send.at[phase, m, group],
            recv_sem=swap_recv.at[phase, m, group],
            device_id=(side * half_el + index, my_tg),
            device_id_type=mesh_id,
        )

    def swapped(phase, m, group):
        side = 1 - my_half if phase == 0 else my_half
        index = lax.rem(my_index + half_el - m, half_el)
        return pltpu.make_async_copy(
            mixed.at[phase, pl.ds(0, per_half), pl.ds(group * piece, piece)],
            out_hbm.at[:, columns(side * half_el + index, group)],
            swap_recv.at[phase, m, group],
        )

    def place(group):
        return pltpu.make_async_copy(
            mixed.at[1, block(my_index), pl.ds(group * piece, piece)],
            out_hbm.at[:, columns(my_el, group)],
            place_sem.at[group],
        )

    weight_copy.wait()
    for phase in range(2):
        land(phase)
        for group in range(GROUPS):
            multiply(phase, group)
            for m in range(phase, half_el):
                swap(phase, m, group).start()
            if phase == 1:
                place(group).start()

    def sent(step, carry):
        send(step, 1).wait_send()
        return carry

    lax.fori_loop(0, n - 1, sent, 0)
    for group in range(GROUPS):
        for phase in range(2):
            for m in range(phase, half_el):
                swap(phase, m, group).wait_send()
                swapped(phase, m, group).wait()
        place(group).wait()


def on_device(n_el, n_tg, field_points, owner_map, send_counts, tile_rows, tile_cols, weights):
    elements, points, channels = field_points.shape
    n = n_el * n_tg
    per_owner = elements // n
    _, tiles, blocks, tile, _ = weights.shape
    half_el = n_el // 2
    smem = pl.BlockSpec(memory_space=pltpu.SMEM)
    vmem = pl.BlockSpec(memory_space=pltpu.VMEM)
    slots = max(16, per_owner)
    anywhere = pl.BlockSpec(memory_space=pl.ANY)
    dma = pltpu.SemaphoreType.DMA
    kind = field_points.dtype
    return pl.pallas_call(
        functools.partial(kernel, n_el, n_tg, per_owner),
        out_shape=jax.ShapeDtypeStruct((channels // n_el, n_el * tiles * tile), kind),
        in_specs=[vmem] * 3 + [smem] + [anywhere] * 2,
        out_specs=anywhere,
        scratch_shapes=[
            pltpu.VMEM((elements, points, channels), kind),
            pltpu.VMEM((tiles, blocks, tile, tile), kind),
            pltpu.VMEM((2, n, per_owner, points, LANES), kind),
            pltpu.VMEM((n, per_owner, points, LANES), kind),
            pltpu.VMEM((n, per_owner, points, LANES), kind),
            pltpu.VMEM((2, LANES, tiles * tile), kind),
            dma(()),
            dma(()),
            dma((2,)),
            dma((2, n)),
            dma((2, n)),
            dma((2, half_el, GROUPS)),
            dma((2, half_el, GROUPS)),
            dma((GROUPS,)),
            pltpu.VMEM((2 * slots, max(n, LANES)), jnp.int32),
            pltpu.VMEM((8, LANES), jnp.int32),
            pltpu.SMEM((2 * slots, max(n, LANES)), jnp.int32),
            pltpu.SMEM((8, LANES), jnp.int32),
            dma((2,)),
        ],
        compiler_params=pltpu.CompilerParams(
            collective_id=0, has_side_effects=True, vmem_limit_bytes=56 * 2**20
        ),
        cost_estimate=pl.CostEstimate(
            flops=2 * tiles * blocks * tile * tile * channels,
            bytes_accessed=weights.size * 2 + field_points.size * 2,
            transcendentals=0,
        ),
    )(owner_map, send_counts, tile_rows, tile_cols[0].T, field_points, weights[0])


def solution(mesh):
    n_el, n_tg = mesh.shape["el"], mesh.shape["tg"]
    return jax.shard_map(
        functools.partial(on_device, n_el, n_tg),
        mesh=mesh,
        in_specs=(
            P(("el", "tg"), None, None),
            P(("el", "tg"), None),
            P(("el", "tg"), None),
            P(("el", "tg"), None),
            P(("el", "tg"), None, None),
            P(("el", "tg"), None, None, None, None),
        ),
        out_specs=P("el", "tg"),
        check_vma=False,
    )
```

```python
import functools

import jax
import jax.numpy as jnp
from jax import lax
from jax.experimental import pallas as pl
from jax.experimental.pallas import tpu as pltpu
from jax.sharding import PartitionSpec as P

LANES = 128
GROUPS = 4
UNROLL = 4


def kernel(
    n_el, n_tg, per_owner, owner_ref, counts_ref, rows_ref, cols_ref, field_hbm, weights_hbm, out_hbm,
    field, weights, packed, source_far, source_near, mixed, field_sem, weight_sem, own_sem, send_sem, recv_sem,
    swap_send, swap_recv, place_sem, table_vmem, place_vmem, table, place_table, table_sem,
):
    n = n_el * n_tg
    half_el = n_el // 2
    mesh_id = pl.DeviceIdType.MESH
    my_el = lax.axis_index("el")
    my_tg = lax.axis_index("tg")
    me = my_el * n_tg + my_tg
    points = field.shape[1]
    tiles, blocks = weights.shape[:2]
    tile = weights.shape[2]
    per_half = LANES // half_el
    cells = tiles * tile
    sources = (source_far, source_near)

    field_copy = pltpu.make_async_copy(field_hbm, field, field_sem)
    field_copy.start()
    weight_copy = pltpu.make_async_copy(weights_hbm, weights, weight_sem)

    barrier = pltpu.get_barrier_semaphore()

    def offsets(step):
        count = step + 1
        return lax.rem(count // n_tg, n_el), lax.rem(count, n_tg)

    def peer(step):
        el_step, tg_step = offsets(step)
        where = (lax.rem(my_el + el_step, n_el), lax.rem(my_tg + tg_step, n_tg))
        return where[0] * n_tg + where[1], where

    def greet(step, carry):
        pl.semaphore_signal(barrier, inc=1, device_id=peer(step)[1], device_id_type=mesh_id)
        return carry

    lax.fori_loop(0, n - 1, greet, 0)

    slots = table_vmem.shape[0] // 2
    elements = field.shape[0]
    owner = owner_ref[...]
    index = lax.broadcasted_iota(jnp.int32, (1, elements), 1)
    owned = lax.broadcasted_iota(jnp.int32, (table_vmem.shape[1], elements), 0) == owner
    onehot = owned.astype(jnp.float32).astype(jnp.bfloat16)
    earlier = lax.broadcasted_iota(jnp.int32, (elements, elements), 0) < lax.broadcasted_iota(
        jnp.int32, (elements, elements), 1
    )
    before = jnp.dot(onehot, earlier.astype(jnp.float32).astype(jnp.bfloat16), preferred_element_type=jnp.float32)
    rank = jnp.sum(jnp.where(owned, before, 0.0), axis=0, keepdims=True).astype(jnp.int32)
    ranked = lax.broadcasted_iota(jnp.int32, (slots, elements), 0) == rank
    picks = [jnp.where(ranked, x, 0).astype(jnp.float32) for x in (index // LANES, lax.rem(index, LANES), counts_ref[...])]
    found = lax.dot_general(
        jnp.concatenate(picks, axis=0).astype(jnp.bfloat16), onehot, (((1,), (1,)), ((), ())),
        preferred_element_type=jnp.float32,
    ).astype(jnp.int32)
    table_vmem[:slots] = found[:slots] * LANES + found[slots:2 * slots]
    table_vmem[slots:] = found[2 * slots:]
    placed = lax.broadcasted_iota(jnp.int32, (place_vmem.shape[1], tiles), 0) == rows_ref[...]
    order = lax.broadcasted_iota(jnp.int32, (place_vmem.shape[0], tiles), 1)
    place_vmem[...] = lax.dot_general(
        order.astype(jnp.float32).astype(jnp.bfloat16), placed.astype(jnp.float32).astype(jnp.bfloat16),
        (((1,), (1,)), ((), ())), preferred_element_type=jnp.float32,
    ).astype(jnp.int32)
    table_copies = [
        pltpu.make_async_copy(table_vmem, table, table_sem.at[0]),
        pltpu.make_async_copy(place_vmem, place_table, table_sem.at[1]),
    ]
    for copy in table_copies:
        copy.start()
    for copy in table_copies:
        copy.wait()
    field_copy.wait()

    row = lax.broadcasted_iota(jnp.int32, (points, LANES), 0)

    def pack(other):
        def one(g, carry):
            element = jnp.clip(table[g, other], 0, elements - 1)
            live = row < table[slots + g, other]
            for h in range(2):
                values = field[element, :, h * LANES:(h + 1) * LANES]
                packed[h, other, g] = jnp.where(live, values, jnp.zeros_like(values))
            return carry

        lax.fori_loop(0, per_owner, one, 0, unroll=min(per_owner, 4))

    def lanes_of(other_el, phase):
        near = other_el // half_el
        return 1 - near if phase == 0 else near

    def send(step, phase):
        other, where = peer(step)
        return pltpu.make_async_remote_copy(
            src_ref=packed.at[lanes_of(where[0], phase), other],
            dst_ref=sources[phase].at[me],
            send_sem=send_sem.at[phase, step],
            recv_sem=recv_sem.at[phase, step],
            device_id=where,
            device_id_type=mesh_id,
        )

    def arrival(step, phase):
        el_step, tg_step = offsets(step)
        sender = lax.rem(my_el + n_el - el_step, n_el) * n_tg + lax.rem(my_tg + n_tg - tg_step, n_tg)
        return pltpu.make_async_copy(packed.at[0, 0], sources[phase].at[sender], recv_sem.at[phase, step])

    pack(peer(0)[0])
    pl.semaphore_wait(barrier, n - 1)

    def first(step, carry):
        send(step, 0).start()
        pack(peer(step + 1)[0])
        return carry

    lax.fori_loop(0, n - 1, first, 0)
    weight_copy.start()
    for phase in range(2):
        pltpu.make_async_copy(packed.at[lanes_of(my_el, phase), me], sources[phase].at[me], own_sem.at[phase]).start()

    def second(step, carry):
        send(step, 0).wait_send()
        send(step, 1).start()
        return carry

    lax.fori_loop(0, n - 1, second, 0)

    def land(phase):
        def landed(step, carry):
            arrival(step, phase).wait()
            return carry

        lax.fori_loop(0, n - 1, landed, 0)
        pltpu.make_async_copy(packed.at[0, 0], sources[phase].at[me], own_sem.at[phase]).wait()

    def multiply(phase, group):
        flat = sources[phase].reshape(n * per_owner * points // tile, tile, LANES)

        def one(q, carry):
            t = jnp.clip(place_table[0, q], 0, tiles - 1)
            left = jnp.concatenate([weights[t, k] for k in range(blocks)], axis=1)
            right = jnp.concatenate([flat[cols_ref[k, t]] for k in range(blocks)], axis=0)
            product = jnp.dot(left, right, preferred_element_type=jnp.float32)
            start = pl.multiple_of(q * tile, tile)
            mixed[phase, :, pl.ds(start, tile)] = product.T.astype(mixed.dtype)
            return carry

        share = tiles // GROUPS
        lax.fori_loop(group * share, (group + 1) * share, one, 0, unroll=UNROLL)

    piece = cells // GROUPS
    my_half = my_el // half_el
    my_index = lax.rem(my_el, half_el)

    def block(index):
        return pl.ds(pl.multiple_of(index * per_half, per_half), per_half)

    def columns(owner_el, group):
        return pl.ds(pl.multiple_of(owner_el * cells + group * piece, piece), piece)

    def swap(phase, m, group):
        side = 1 - my_half if phase == 0 else my_half
        index = lax.rem(my_index + m, half_el)
        return pltpu.make_async_remote_copy(
            src_ref=mixed.at[phase, block(index), pl.ds(group * piece, piece)],
            dst_ref=out_hbm.at[:, columns(my_el, group)],
            send_sem=swap_send.at[phase, m, group],
            recv_sem=swap_recv.at[phase, m, group],
            device_id=(side * half_el + index, my_tg),
            device_id_type=mesh_id,
        )

    def swapped(phase, m, group):
        side = 1 - my_half if phase == 0 else my_half
        index = lax.rem(my_index + half_el - m, half_el)
        return pltpu.make_async_copy(
            mixed.at[phase, pl.ds(0, per_half), pl.ds(group * piece, piece)],
            out_hbm.at[:, columns(side * half_el + index, group)],
            swap_recv.at[phase, m, group],
        )

    def place(group):
        return pltpu.make_async_copy(
            mixed.at[1, block(my_index), pl.ds(group * piece, piece)],
            out_hbm.at[:, columns(my_el, group)],
            place_sem.at[group],
        )

    weight_copy.wait()
    for phase in range(2):
        land(phase)
        for group in range(GROUPS):
            multiply(phase, group)
            for m in range(phase, half_el):
                swap(phase, m, group).start()
            if phase == 1:
                place(group).start()

    def sent(step, carry):
        send(step, 1).wait_send()
        return carry

    lax.fori_loop(0, n - 1, sent, 0)
    for group in range(GROUPS):
        for phase in range(2):
            for m in range(phase, half_el):
                swap(phase, m, group).wait_send()
                swapped(phase, m, group).wait()
        place(group).wait()


def on_device(n_el, n_tg, field_points, owner_map, send_counts, tile_rows, tile_cols, weights):
    elements, points, channels = field_points.shape
    n = n_el * n_tg
    per_owner = elements // n
    _, tiles, blocks, tile, _ = weights.shape
    half_el = n_el // 2
    smem = pl.BlockSpec(memory_space=pltpu.SMEM)
    vmem = pl.BlockSpec(memory_space=pltpu.VMEM)
    slots = max(16, per_owner)
    anywhere = pl.BlockSpec(memory_space=pl.ANY)
    dma = pltpu.SemaphoreType.DMA
    kind = field_points.dtype
    return pl.pallas_call(
        functools.partial(kernel, n_el, n_tg, per_owner),
        out_shape=pltpu.VMEM((channels // n_el, n_el * tiles * tile), kind),
        in_specs=[vmem] * 3 + [smem] + [anywhere] * 2,
        out_specs=vmem,
        scratch_shapes=[
            pltpu.VMEM((elements, points, channels), kind),
            pltpu.VMEM((tiles, blocks, tile, tile), kind),
            pltpu.VMEM((2, n, per_owner, points, LANES), kind),
            pltpu.VMEM((n, per_owner, points, LANES), kind),
            pltpu.VMEM((n, per_owner, points, LANES), kind),
            pltpu.VMEM((2, LANES, tiles * tile), kind),
            dma(()),
            dma(()),
            dma((2,)),
            dma((2, n)),
            dma((2, n)),
            dma((2, half_el, GROUPS)),
            dma((2, half_el, GROUPS)),
            dma((GROUPS,)),
            pltpu.VMEM((2 * slots, max(n, LANES)), jnp.int32),
            pltpu.VMEM((8, LANES), jnp.int32),
            pltpu.SMEM((2 * slots, max(n, LANES)), jnp.int32),
            pltpu.SMEM((8, LANES), jnp.int32),
            dma((2,)),
        ],
        compiler_params=pltpu.CompilerParams(
            collective_id=0, has_side_effects=True, vmem_limit_bytes=56 * 2**20
        ),
        cost_estimate=pl.CostEstimate(
            flops=2 * tiles * blocks * tile * tile * channels,
            bytes_accessed=weights.size * 2 + field_points.size * 2,
            transcendentals=0,
        ),
    )(owner_map, send_counts, tile_rows, tile_cols[0].T, field_points, weights[0])


def solution(mesh):
    n_el, n_tg = mesh.shape["el"], mesh.shape["tg"]
    return jax.shard_map(
        functools.partial(on_device, n_el, n_tg),
        mesh=mesh,
        in_specs=(
            P(("el", "tg"), None, None),
            P(("el", "tg"), None),
            P(("el", "tg"), None),
            P(("el", "tg"), None),
            P(("el", "tg"), None, None),
            P(("el", "tg"), None, None, None, None),
        ),
        out_specs=P("el", "tg"),
        check_vma=False,
    )
```
